32 devices in a mesh: row: 4 (over y, x), col: 8 (over z, core).
Axes of the slice: x: 2, y: 2, z: 4, core: 2. Of those that a mesh axis runs over, the one named last changes fastest.
Arguments:
- latent: bfloat16 [16, 131072], P(None, ('row', 'col')), may hold values from -200 to 200, as said below
- in_weight: bfloat16 [3, 3, 16, 512], replicated, may hold values from -0.5 to 0.5
- in_bias: float32 [512], replicated, may hold values from -3 to 3
- norm_gain: float32 [512], replicated, may hold values from 0.25 to 1.75
- norm_shift: float32 [512], replicated, may hold values from -3 to 3
- mid_weight: bfloat16 [512, 3, 3, 512], replicated, may hold values from -0.09375 to 0.09375
- mid_bias: float32 [512], replicated, may hold values from -3 to 3
Outputs:
- features: bfloat16 [256, 512, 512], P('row', 'col')
The draws below stay inside these ranges and needn't reach their ends.
Inputs may be any that keep to these rules, and one draw needn't show every extreme that they name: real-valued latent entries.
All inputs are finite; a program needn't handle non-finite values.
Results may differ from the reference program's by a relative error of at most 0.0095.
Values may be sent and summed in bfloat16 or wider, within the bound.
A program may use at most 192 MiB of HBM per device.

```python
import jax
import jax.numpy as jnp
from jax import lax

C_LAT = 16
CH = 512
GROUPS = 32
TILE_H = 64
TILE_W = 64
N_ROW = 4
N_COL = 8


def draw_latent(key, part):
    first_key, second_key, third_key = jax.random.split(jax.random.fold_in(key, 11), 3)
    height = TILE_H * N_ROW
    breadth = TILE_W * N_COL
    ramp = jnp.arange(height, dtype=jnp.float32) / (height - 1)
    values = jnp.clip(jax.random.normal(first_key, (C_LAT, height, breadth), jnp.float32), -4.0, 4.0)
    values = values + (0.5 + ramp)[None, :, None]
    row_scale = jnp.exp(ramp * 1.0986) * jax.random.uniform(second_key, (height,), jnp.float32, 0.7, 1.3)
    col_scale = jax.random.uniform(third_key, (breadth,), jnp.float32, 0.7, 1.3)
    field = values * row_scale[None, :, None] * col_scale[None, None, :]
    return field.reshape(C_LAT, height * breadth).astype(jnp.bfloat16)


def gaussian(stream_key, shape, spread, reach, kind=jnp.bfloat16):
    result = spread * jax.random.normal(stream_key, shape, jnp.float32)
    return jnp.clip(result, min=-reach, max=reach).astype(kind)


def setup_inputs(seed: int = 0) -> dict:
    keys = jax.random.split(jax.random.key(seed), 8)
    latent = draw_latent(jax.random.fold_in(keys[7], 71), 0)
    in_weight = gaussian(keys[1], (3, 3, C_LAT, CH), (9 * C_LAT) ** -0.5, 0.5)
    in_bias = gaussian(keys[2], (CH,), 0.5, 3.0, jnp.float32)
    norm_gain = jnp.clip(1.0 + 0.15 * jax.random.normal(keys[3], (CH,), jnp.float32), 0.25, 1.75)
    norm_shift = gaussian(keys[4], (CH,), 0.5, 3.0, jnp.float32)
    mid_weight = gaussian(keys[5], (CH, 3, 3, CH), (9 * CH) ** -0.5, 0.09375)
    mid_bias = gaussian(keys[6], (CH,), 0.5, 3.0, jnp.float32)
    return {"latent": latent, "in_weight": in_weight, "in_bias": in_bias, "norm_gain": norm_gain, "norm_shift": norm_shift, "mid_weight": mid_weight, "mid_bias": mid_bias}


EPSILON = 1e-06

def reference(latent, in_weight, in_bias, norm_gain, norm_shift, mid_weight, mid_bias):
    height = TILE_H * N_ROW
    breadth = TILE_W * N_COL
    picture = latent.reshape(1, C_LAT, height, breadth)
    first_out = lax.conv_general_dilated(picture, in_weight, (1, 1), ((1, 1), (1, 1)), dimension_numbers=('NCHW', 'HWIO', 'NHWC'), preferred_element_type=jnp.float32)[0]
    first_out = (first_out + in_bias).astype(jnp.bfloat16)
    grouped = first_out.astype(jnp.float32).reshape(height * breadth, GROUPS, CH // GROUPS)
    cells = height * breadth * (CH // GROUPS)
    group_mean = lax.optimization_barrier(jnp.sum(grouped, axis=(0, 2))) / cells
    centred = grouped - group_mean[None, :, None]
    group_var = lax.optimization_barrier(jnp.sum(centred * centred, axis=(0, 2))) / cells
    normed = centred * lax.rsqrt(group_var + EPSILON)[None, :, None]
    normed = normed.reshape(height, breadth, CH) * norm_gain + norm_shift
    activated = jax.nn.silu(normed).astype(jnp.bfloat16)
    features = lax.conv_general_dilated(activated[None], mid_weight, (1, 1), ((1, 1), (1, 1)), dimension_numbers=('NHWC', 'OHWI', 'NHWC'), preferred_element_type=jnp.float32)[0]
    return (features + mid_bias).astype(jnp.bfloat16)
```

```python
import functools

import jax
import jax.numpy as jnp
from jax import lax
from jax.experimental import pallas as pl
from jax.experimental.pallas import tpu as pltpu
from jax.sharding import PartitionSpec as P

GROUPS = 32
TILE_W = 64
EPSILON = 1e-06
LANES = 128
MESH = pl.DeviceIdType.MESH
COLS_PAD = 80
ROWS_STEP = 4


def front_kernel(
    n_row, n_col, lat_ref, w_ref, bias_ref, gain_ref, shift_ref,
    fo_ref, ss_ref,
    send, x_ref, xs_ref, part, slot_col, part_row, slot_row,
    send_sem, recv_sem, halo_send, halo_recv, s1_send, s1_recv, s2_send, s2_recv,
):
    row, col = lax.axis_index("row"), lax.axis_index("col")
    c_lat = lat_ref.shape[0]
    breadth = TILE_W * n_col
    rp = lat_ref.shape[1] // breadth
    tile_h = rp * n_col

    barrier = pltpu.get_barrier_semaphore()
    for k in range(1, n_col):
        pl.semaphore_signal(
            barrier, inc=1, device_id=(row, lax.rem(col + k, n_col)), device_id_type=MESH
        )
    for k in range(1, n_row):
        pl.semaphore_signal(
            barrier, inc=1, device_id=(lax.rem(row + k, n_row), col), device_id_type=MESH
        )

    zero_tile = jnp.zeros((c_lat, LANES), jnp.float32)
    for r in range(rp):
        tiles = [
            lat_ref[:, r * breadth + t * LANES : r * breadth + (t + 1) * LANES].astype(jnp.float32)
            for t in range(breadth // LANES)
        ]
        for c in range(n_col):
            start = c * TILE_W - 2
            t0 = start // LANES
            off = start - t0 * LANES
            lo = tiles[t0] if t0 >= 0 else zero_tile
            hi = tiles[t0 + 1] if t0 + 1 < len(tiles) else zero_tile
            both = pltpu.roll(jnp.concatenate([lo, hi], axis=1), 2 * LANES - off, 1)
            send[c, r * c_lat : (r + 1) * c_lat, :] = both[:, :LANES].astype(jnp.bfloat16)

    pl.semaphore_wait(barrier, n_col + n_row - 2)

    def rows(first, count):
        return pl.ds(pl.multiple_of(first * c_lat, c_lat), count * c_lat)

    mine = rows(2 + col * rp, rp)
    copies = []
    for k in range(1, n_col):
        target = lax.rem(col + k, n_col)
        copy = pltpu.make_async_remote_copy(
            src_ref=send.at[target],
            dst_ref=x_ref.at[mine],
            send_sem=send_sem.at[k],
            recv_sem=recv_sem.at[k],
            device_id=(row, target),
            device_id_type=MESH,
        )
        copy.start()
        copies.append(copy)
    x_ref[mine, :] = send[col]

    @pl.when(row == 0)
    def _():
        x_ref[rows(0, 2), :] = jnp.zeros((2 * c_lat, LANES), jnp.bfloat16)

    @pl.when(row == n_row - 1)
    def _():
        x_ref[rows(tile_h + 2, 2), :] = jnp.zeros((2 * c_lat, LANES), jnp.bfloat16)

    for copy in copies:
        copy.wait_recv()

    down = pltpu.make_async_remote_copy(
        src_ref=x_ref.at[rows(tile_h, 2)],
        dst_ref=x_ref.at[rows(0, 2)],
        send_sem=halo_send.at[0],
        recv_sem=halo_recv.at[0],
        device_id=(jnp.minimum(row + 1, n_row - 1), col),
        device_id_type=MESH,
    )
    up = pltpu.make_async_remote_copy(
        src_ref=x_ref.at[rows(2, 2)],
        dst_ref=x_ref.at[rows(tile_h + 2, 2)],
        send_sem=halo_send.at[1],
        recv_sem=halo_recv.at[1],
        device_id=(jnp.maximum(row - 1, 0), col),
        device_id_type=MESH,
    )

    @pl.when(row < n_row - 1)
    def _():
        down.start()

    @pl.when(row > 0)
    def _():
        up.start()

    def spread(i):
        src = x_ref[rows(i, 1), :].astype(jnp.float32)
        for b in range(3):
            moved = src if b == 0 else pltpu.roll(src, LANES - b, 1)
            xs_ref[rows(3 * i + b, 1), :] = moved.astype(jnp.bfloat16)

    def spread_loop(i, carry):
        for u in range(4):
            spread(2 + i * 4 + u)
        return carry

    lax.fori_loop(0, tile_h // 4, spread_loop, 0)

    cell = lax.broadcasted_iota(jnp.int32, (COLS_PAD, 1), 0)
    inside = jnp.logical_and(cell >= 1, cell <= TILE_W)
    weight = w_ref[...]
    bias = bias_ref[...]
    channels = weight.shape[1]

    def conv_row(i):
        patch = xs_ref[rows(3 * i, 9), :]
        out = lax.dot_general(
            patch, weight, (((0,), (0,)), ((), ())), preferred_element_type=jnp.float32
        )[:COLS_PAD]
        out = (out + bias).astype(jnp.bfloat16)
        fo_ref[i] = out
        return out

    def stats_row(i, carry):
        total, squares = carry
        out = jnp.where(inside, conv_row(i).astype(jnp.float32), 0.0)
        grouped = out.reshape(COLS_PAD // 8, 8, channels)
        return total + jnp.sum(grouped, axis=0), squares + jnp.sum(grouped * grouped, axis=0)

    def stats_pair(i, carry):
        return stats_row(3 + 2 * i, stats_row(2 + 2 * i, carry))

    zero = jnp.zeros((8, channels), jnp.float32)
    carry = lax.fori_loop(0, (tile_h - 2) // 2, stats_pair, (zero, zero))

    @pl.when(row < n_row - 1)
    def _():
        up.wait_recv()

    @pl.when(row > 0)
    def _():
        down.wait_recv()

    for i in (0, 1, tile_h + 2, tile_h + 3):
        spread(i)
    carry = stats_row(tile_h, stats_row(1, carry))
    part[0:1, :] = jnp.sum(carry[0], axis=0, keepdims=True)
    part[1:2, :] = jnp.sum(carry[1], axis=0, keepdims=True)

    firsts = []
    for k in range(1, n_col):
        copy = pltpu.make_async_remote_copy(
            src_ref=part, dst_ref=slot_col.at[k], send_sem=s1_send.at[k],
            recv_sem=s1_recv.at[k],
            device_id=(row, lax.rem(col + k, n_col)), device_id_type=MESH,
        )
        copy.start()
        firsts.append(copy)
    conv_row(0)
    conv_row(tile_h + 1)
    acc = part[...]
    for k, copy in enumerate(firsts):
        copy.wait_recv()
        acc = acc + slot_col[k + 1]
    part_row[...] = acc
    seconds = []
    for k in range(1, n_row):
        copy = pltpu.make_async_remote_copy(
            src_ref=part_row, dst_ref=slot_row.at[k], send_sem=s2_send.at[k],
            recv_sem=s2_recv.at[k],
            device_id=(lax.rem(row + k, n_row), col), device_id_type=MESH,
        )
        copy.start()
        seconds.append(copy)
    for k, copy in enumerate(seconds):
        copy.wait_recv()
        acc = acc + slot_row[k + 1]

    width = channels // GROUPS
    left = lax.broadcasted_iota(jnp.int32, (channels, channels), 0) // width
    right = lax.broadcasted_iota(jnp.int32, (channels, channels), 1) // width
    same = (left == right).astype(jnp.float32)
    padded = jnp.concatenate([acc, jnp.zeros((6, channels), jnp.float32)], axis=0)
    summed = jnp.dot(
        padded, same, precision=lax.Precision.HIGHEST, preferred_element_type=jnp.float32
    )
    cells = float(tile_h * TILE_W * n_row * n_col * width)
    mean = summed[0:1] / cells
    var = summed[1:2] / cells - mean * mean
    scale = lax.rsqrt(var + EPSILON) * gain_ref[...]
    ss_ref[0:1, :] = scale
    ss_ref[1:2, :] = shift_ref[...] - mean * scale

    for copy in copies + firsts + seconds:
        copy.wait_send()

    @pl.when(row < n_row - 1)
    def _():
        down.wait_send()

    @pl.when(row > 0)
    def _():
        up.wait_send()


def mid_kernel(n_row, n_col, tile_h, fo_ref, ss_ref, w_ref, bias_ref, out_ref, act_ref):
    row, col = lax.axis_index("row"), lax.axis_index("col")
    step = pl.program_id(0)
    channels = fo_ref.shape[2]
    scale = ss_ref[0:1, :] * 0.5
    shift = ss_ref[1:2, :] * 0.5
    cell = lax.broadcasted_iota(jnp.int32, (COLS_PAD, 1), 0)
    lowest = jnp.where(col == 0, 1, 0)
    highest = jnp.where(col == n_col - 1, TILE_W, TILE_W + 1)
    inside = jnp.logical_and(cell >= lowest, cell <= highest)

    def activate(i):
        half = fo_ref[i].astype(jnp.float32) * scale + shift
        value = half + half * jnp.tanh(half)
        beyond = jnp.logical_or(
            jnp.logical_and(row == 0, i == 0),
            jnp.logical_and(row == n_row - 1, i == tile_h + 1),
        )
        value = jnp.where(jnp.logical_and(inside, jnp.logical_not(beyond)), value, 0.0)
        first = pl.multiple_of(i * TILE_W, TILE_W)
        for b in range(3):
            moved = value if b == 0 else pltpu.roll(value, COLS_PAD - b, 0)
            act_ref[pl.ds(first, TILE_W), b * channels : (b + 1) * channels] = moved[
                :TILE_W
            ].astype(jnp.bfloat16)

    @pl.when(step == 0)
    def _():
        activate(0)
        activate(1)

    for u in range(ROWS_STEP):
        activate(step * ROWS_STEP + 2 + u)

    rows_m = ROWS_STEP * TILE_W
    acc = None
    for a in range(3):
        lhs = act_ref[pl.ds(pl.multiple_of((step * ROWS_STEP + a) * TILE_W, TILE_W), rows_m), :]
        rhs = jnp.concatenate([w_ref[3 * a + b] for b in range(3)], axis=1)
        prod = lax.dot_general(
            lhs, rhs, (((1,), (1,)), ((), ())), preferred_element_type=jnp.float32
        )
        acc = prod if acc is None else acc + prod
    out_ref[...] = (acc + bias_ref[...]).astype(jnp.bfloat16).reshape(out_ref.shape)


def body(n_row, n_col, latent, in_weight, in_bias, norm_gain, norm_shift, mid_weight, mid_bias):
    c_lat = latent.shape[0]
    channels = in_bias.shape[0]
    rp = latent.shape[1] // (TILE_W * n_col)
    tile_h = rp * n_col
    vmem = pl.BlockSpec(memory_space=pltpu.VMEM)
    dma = pltpu.SemaphoreType.DMA
    fo, ss = pl.pallas_call(
        functools.partial(front_kernel, n_row, n_col),
        out_shape=(
            jax.ShapeDtypeStruct((tile_h + 2, COLS_PAD, channels), jnp.bfloat16),
            jax.ShapeDtypeStruct((2, channels), jnp.float32),
        ),
        in_specs=[vmem] * 5,
        out_specs=(vmem, vmem),
        scratch_shapes=[
            pltpu.VMEM((n_col, rp * c_lat, LANES), jnp.bfloat16),
            pltpu.VMEM(((tile_h + 4) * c_lat, LANES), jnp.bfloat16),
            pltpu.VMEM(((tile_h + 4) * 3 * c_lat, LANES), jnp.bfloat16),
            pltpu.VMEM((2, channels), jnp.float32),
            pltpu.VMEM((n_col, 2, channels), jnp.float32),
            pltpu.VMEM((2, channels), jnp.float32),
            pltpu.VMEM((n_row, 2, channels), jnp.float32),
            dma((n_col,)), dma((n_col,)), dma((2,)), dma((2,)),
            dma((n_col,)), dma((n_col,)), dma((n_row,)), dma((n_row,)),
        ],
        compiler_params=pltpu.CompilerParams(
            collective_id=0, has_side_effects=True, vmem_limit_bytes=32 * 2**20
        ),
    )(
        latent,
        in_weight.reshape(9 * c_lat, channels),
        in_bias.reshape(1, channels),
        norm_gain.reshape(1, channels),
        norm_shift.reshape(1, channels),
    )
    weight = jnp.transpose(mid_weight, (1, 2, 0, 3)).reshape(9, channels, channels)
    whole = lambda *shape: pl.BlockSpec(shape, lambda s: (0,) * len(shape))
    return pl.pallas_call(
        functools.partial(mid_kernel, n_row, n_col, tile_h),
        grid=(tile_h // ROWS_STEP,),
        out_shape=jax.ShapeDtypeStruct((tile_h, TILE_W, channels), jnp.bfloat16),
        in_specs=[
            whole(tile_h + 2, COLS_PAD, channels),
            whole(2, channels),
            whole(9, channels, channels),
            whole(1, channels),
        ],
        out_specs=pl.BlockSpec((ROWS_STEP, TILE_W, channels), lambda s: (s, 0, 0)),
        scratch_shapes=[pltpu.VMEM(((tile_h + 2) * TILE_W, 3 * channels), jnp.bfloat16)],
        compiler_params=pltpu.CompilerParams(vmem_limit_bytes=56 * 2**20),
        cost_estimate=pl.CostEstimate(
            flops=2 * tile_h * TILE_W * 9 * channels * channels,
            bytes_accessed=14 * 2**20, transcendentals=0,
        ),
    )(fo, ss, weight, mid_bias.reshape(1, channels))


def solution(mesh):
    placed = (P(None, ("row", "col")), P(), P(), P(), P(), P(), P())
    return jax.shard_map(
        functools.partial(body, mesh.shape["row"], mesh.shape["col"]),
        mesh=mesh, in_specs=placed, out_specs=P("row", "col", None), check_vma=False,
    )
```

```python
import functools

import jax
import jax.numpy as jnp
from jax import lax
from jax.experimental import pallas as pl
from jax.experimental.pallas import tpu as pltpu
from jax.sharding import PartitionSpec as P

GROUPS = 32
TILE_W = 64
EPSILON = 1e-06
LANES = 128
MESH = pl.DeviceIdType.MESH
COLS_PAD = 80
COLS_USED = 72
ROWS_STEP = 8


def kernel(
    n_row, n_col, lat_hbm, w_hbm, bias_hbm, gain_hbm, shift_hbm, mid_hbm, mid_bias_hbm,
    out_hbm,
    fo_ref, ss_ref, mid_ref, out_ref, even_ref, odd_ref, out_sem,
    lat_ref, w_ref, bias_ref, gain_ref, shift_ref, mid_bias_ref, fetch_sem,
    send, x_ref, xs_ref, part, slot_col, part_row, slot_row,
    send_sem, recv_sem, halo_send, halo_recv, s1_send, s1_recv, s2_send, s2_recv,
):
    row, col = lax.axis_index("row"), lax.axis_index("col")
    fetches = [
        pltpu.make_async_copy(src, dst, fetch_sem.at[i])
        for i, (src, dst) in enumerate([
            (lat_hbm, lat_ref), (w_hbm, w_ref), (bias_hbm, bias_ref), (gain_hbm, gain_ref),
            (shift_hbm, shift_ref), (mid_bias_hbm, mid_bias_ref), (mid_hbm, mid_ref),
        ])
    ]
    for fetch in fetches:
        fetch.start()
    c_lat = lat_ref.shape[0]
    breadth = TILE_W * n_col
    rp = lat_ref.shape[1] // breadth
    tile_h = rp * n_col

    barrier = pltpu.get_barrier_semaphore()
    for k in range(1, n_col):
        pl.semaphore_signal(
            barrier, inc=1, device_id=(row, lax.rem(col + k, n_col)), device_id_type=MESH
        )
    for k in range(1, n_row):
        pl.semaphore_signal(
            barrier, inc=1, device_id=(lax.rem(row + k, n_row), col), device_id_type=MESH
        )

    fetches[0].wait()
    zero_tile = jnp.zeros((c_lat, LANES), jnp.float32)
    for r in range(rp):
        tiles = [
            lat_ref[:, r * breadth + t * LANES : r * breadth + (t + 1) * LANES].astype(jnp.float32)
            for t in range(breadth // LANES)
        ]
        for c in range(n_col):
            start = c * TILE_W - 2
            t0 = start // LANES
            off = start - t0 * LANES
            lo = tiles[t0] if t0 >= 0 else zero_tile
            hi = tiles[t0 + 1] if t0 + 1 < len(tiles) else zero_tile
            both = pltpu.roll(jnp.concatenate([lo, hi], axis=1), 2 * LANES - off, 1)
            send[c, r * c_lat : (r + 1) * c_lat, :] = both[:, :LANES].astype(jnp.bfloat16)

    pl.semaphore_wait(barrier, n_col + n_row - 2)

    def rows(first, count):
        return pl.ds(pl.multiple_of(first * c_lat, c_lat), count * c_lat)

    mine = rows(2 + col * rp, rp)
    copies = []
    for k in range(1, n_col):
        target = lax.rem(col + k, n_col)
        copy = pltpu.make_async_remote_copy(
            src_ref=send.at[target],
            dst_ref=x_ref.at[mine],
            send_sem=send_sem.at[k],
            recv_sem=recv_sem.at[k],
            device_id=(row, target),
            device_id_type=MESH,
        )
        copy.start()
        copies.append(copy)
    x_ref[mine, :] = send[col]

    @pl.when(row == 0)
    def _():
        x_ref[rows(0, 2), :] = jnp.zeros((2 * c_lat, LANES), jnp.bfloat16)

    @pl.when(row == n_row - 1)
    def _():
        x_ref[rows(tile_h + 2, 2), :] = jnp.zeros((2 * c_lat, LANES), jnp.bfloat16)

    for copy in copies:
        copy.wait_recv()

    down = pltpu.make_async_remote_copy(
        src_ref=x_ref.at[rows(tile_h, 2)],
        dst_ref=x_ref.at[rows(0, 2)],
        send_sem=halo_send.at[0],
        recv_sem=halo_recv.at[0],
        device_id=(jnp.minimum(row + 1, n_row - 1), col),
        device_id_type=MESH,
    )
    up = pltpu.make_async_remote_copy(
        src_ref=x_ref.at[rows(2, 2)],
        dst_ref=x_ref.at[rows(tile_h + 2, 2)],
        send_sem=halo_send.at[1],
        recv_sem=halo_recv.at[1],
        device_id=(jnp.maximum(row - 1, 0), col),
        device_id_type=MESH,
    )

    @pl.when(row < n_row - 1)
    def _():
        down.start()

    @pl.when(row > 0)
    def _():
        up.start()

    def spread(i):
        src = x_ref[rows(i, 1), :].astype(jnp.float32)
        for b in range(3):
            moved = src if b == 0 else pltpu.roll(src, LANES - b, 1)
            xs_ref[rows(3 * i + b, 1), :] = moved.astype(jnp.bfloat16)

    def spread_loop(i, carry):
        for u in range(4):
            spread(2 + i * 4 + u)
        return carry

    lax.fori_loop(0, tile_h // 4, spread_loop, 0)

    fetches[1].wait()
    fetches[2].wait()
    cell = lax.broadcasted_iota(jnp.int32, (COLS_PAD, 1), 0)
    inside = jnp.logical_and(cell >= 1, cell <= TILE_W)
    weight = w_ref[...]
    bias = bias_ref[...]
    channels = weight.shape[1]

    def conv_row(i):
        patch = xs_ref[rows(3 * i, 9), :]
        out = lax.dot_general(
            patch, weight, (((0,), (0,)), ((), ())), preferred_element_type=jnp.float32
        )[:COLS_PAD]
        out = (out + bias).astype(jnp.bfloat16)
        fo_ref[i] = out
        return out

    def stats_row(i, carry):
        total, squares = carry
        out = jnp.where(inside, conv_row(i).astype(jnp.float32), 0.0)
        grouped = out.reshape(COLS_PAD // 8, 8, channels)
        return total + jnp.sum(grouped, axis=0), squares + jnp.sum(grouped * grouped, axis=0)

    def stats_pair(i, carry):
        return stats_row(3 + 2 * i, stats_row(2 + 2 * i, carry))

    zero = jnp.zeros((8, channels), jnp.float32)
    carry = lax.fori_loop(0, (tile_h - 2) // 2, stats_pair, (zero, zero))

    @pl.when(row < n_row - 1)
    def _():
        up.wait_recv()

    @pl.when(row > 0)
    def _():
        down.wait_recv()

    for i in (0, 1, tile_h + 2, tile_h + 3):
        spread(i)
    carry = stats_row(tile_h, stats_row(1, carry))
    part[0:1, :] = jnp.sum(carry[0], axis=0, keepdims=True)
    part[1:2, :] = jnp.sum(carry[1], axis=0, keepdims=True)

    for fetch in fetches[3:]:
        fetch.wait()
    firsts = []
    for k in range(1, n_col):
        copy = pltpu.make_async_remote_copy(
            src_ref=part, dst_ref=slot_col.at[k], send_sem=s1_send.at[k],
            recv_sem=s1_recv.at[k],
            device_id=(row, lax.rem(col + k, n_col)), device_id_type=MESH,
        )
        copy.start()
        firsts.append(copy)
    conv_row(0)
    conv_row(tile_h + 1)
    acc = part[...]
    for k, copy in enumerate(firsts):
        copy.wait_recv()
        acc = acc + slot_col[k + 1]
    part_row[...] = acc
    seconds = []
    for k in range(1, n_row):
        copy = pltpu.make_async_remote_copy(
            src_ref=part_row, dst_ref=slot_row.at[k], send_sem=s2_send.at[k],
            recv_sem=s2_recv.at[k],
            device_id=(lax.rem(row + k, n_row), col), device_id_type=MESH,
        )
        copy.start()
        seconds.append(copy)
    for k, copy in enumerate(seconds):
        copy.wait_recv()
        acc = acc + slot_row[k + 1]

    width = channels // GROUPS
    left = lax.broadcasted_iota(jnp.int32, (channels, channels), 0) // width
    right = lax.broadcasted_iota(jnp.int32, (channels, channels), 1) // width
    same = (left == right).astype(jnp.float32)
    padded = jnp.concatenate([acc, jnp.zeros((6, channels), jnp.float32)], axis=0)
    summed = jnp.dot(
        padded, same, precision=lax.Precision.HIGHEST, preferred_element_type=jnp.float32
    )
    cells = float(tile_h * TILE_W * n_row * n_col * width)
    mean = summed[0:1] / cells
    var = summed[1:2] / cells - mean * mean
    scale = lax.rsqrt(var + EPSILON) * gain_ref[...]
    ss_ref[0:1, :] = scale
    ss_ref[1:2, :] = shift_ref[...] - mean * scale
    mid_conv(
        n_row, n_col, tile_h, fo_ref, ss_ref, mid_ref, mid_bias_ref, out_ref, out_hbm,
        even_ref, odd_ref, out_sem,
    )

    for copy in copies + firsts + seconds:
        copy.wait_send()

    @pl.when(row < n_row - 1)
    def _():
        down.wait_send()

    @pl.when(row > 0)
    def _():
        up.wait_send()


def mid_conv(
    n_row, n_col, tile_h, fo_ref, ss_ref, w_ref, bias_ref, out_ref, out_hbm,
    even_ref, odd_ref, out_sem,
):
    row, col = lax.axis_index("row"), lax.axis_index("col")
    channels = fo_ref.shape[2]
    scale = ss_ref[0:1, :] * 0.5
    shift = ss_ref[1:2, :] * 0.5
    bias = bias_ref[...]
    cell = lax.broadcasted_iota(jnp.int32, (COLS_USED, 1), 0)
    lowest = jnp.where(col == 0, 1, 0)
    highest = jnp.where(col == n_col - 1, TILE_W, TILE_W + 1)

    def activate(i, act_ref, slot):
        half = fo_ref[i, :COLS_USED].astype(jnp.float32) * scale + shift
        value = half + half * jnp.tanh(half)
        beyond = jnp.logical_or(
            jnp.logical_and(row == 0, i == 0),
            jnp.logical_and(row == n_row - 1, i == tile_h + 1),
        )
        last = jnp.where(beyond, -1, highest)
        value = jnp.where(jnp.logical_and(cell >= lowest, cell <= last), value, 0.0)
        for b in range(3):
            moved = value if b == 0 else pltpu.roll(value, COLS_USED - b, 0)
            act_ref[slot * TILE_W : (slot + 1) * TILE_W, b * channels : (b + 1) * channels] = (
                moved[:TILE_W].astype(jnp.bfloat16)
            )

    for i in range(ROWS_STEP + 2):
        activate(i, even_ref, i)

    rows_m = ROWS_STEP * TILE_W
    blocks = tile_h // ROWS_STEP

    def leave(block):
        part = pl.ds(block * ROWS_STEP, ROWS_STEP)
        return pltpu.make_async_copy(out_ref.at[part], out_hbm.at[part], out_sem.at[block])

    def two_blocks(step, carry):
        for half_step, (now, later) in enumerate(((even_ref, odd_ref), (odd_ref, even_ref))):
            first = (2 * step + half_step + 1) * ROWS_STEP
            later[: 2 * TILE_W, :] = now[rows_m:, :]
            acc = None
            done = 0
            for a in range(3):
                rhs = jnp.concatenate([w_ref[3 * a + b] for b in range(3)], axis=1)
                prod = lax.dot_general(
                    now[a * TILE_W : a * TILE_W + rows_m, :], rhs, (((1,), (1,)), ((), ())),
                    preferred_element_type=jnp.float32,
                )
                upto = ((a + 1) * ROWS_STEP) // 3
                for u in range(done, upto):
                    activate(jnp.minimum(first + 2 + u, tile_h + 1), later, 2 + u)
                done = upto
                acc = prod if acc is None else acc + prod
            out_ref[pl.ds(first - ROWS_STEP, ROWS_STEP)] = (
                (acc + bias).astype(jnp.bfloat16).reshape(ROWS_STEP, TILE_W, channels)
            )
            leave(2 * step + half_step).start()
        return carry

    lax.fori_loop(0, blocks // 2, two_blocks, 0)
    for block in range(blocks):
        leave(block).wait()


def body(n_row, n_col, latent, in_weight, in_bias, norm_gain, norm_shift, mid_weight, mid_bias):
    c_lat = latent.shape[0]
    channels = in_bias.shape[0]
    rp = latent.shape[1] // (TILE_W * n_col)
    tile_h = rp * n_col
    dma = pltpu.SemaphoreType.DMA
    vector = pltpu.VMEM((1, channels), jnp.float32)
    weight = jnp.transpose(mid_weight, (1, 2, 0, 3)).reshape(9, channels, channels)
    act = pltpu.VMEM(((ROWS_STEP + 2) * TILE_W, 3 * channels), jnp.bfloat16)
    out_shape = (tile_h, TILE_W, channels)
    hbm = pl.BlockSpec(memory_space=pltpu.HBM)
    return pl.pallas_call(
        functools.partial(kernel, n_row, n_col),
        out_shape=jax.ShapeDtypeStruct(out_shape, jnp.bfloat16),
        in_specs=[hbm] * 7,
        out_specs=hbm,
        scratch_shapes=[
            pltpu.VMEM((tile_h + 2, COLS_PAD, channels), jnp.bfloat16),
            pltpu.VMEM((8, channels), jnp.float32),
            pltpu.VMEM(weight.shape, jnp.bfloat16),
            pltpu.VMEM(out_shape, jnp.bfloat16),
            act, act, dma((tile_h // ROWS_STEP,)),
            pltpu.VMEM(latent.shape, jnp.bfloat16),
            pltpu.VMEM((9 * c_lat, channels), jnp.bfloat16),
            vector, vector, vector, vector, dma((7,)),
            pltpu.VMEM((n_col, rp * c_lat, LANES), jnp.bfloat16),
            pltpu.VMEM(((tile_h + 4) * c_lat, LANES), jnp.bfloat16),
            pltpu.VMEM(((tile_h + 4) * 3 * c_lat, LANES), jnp.bfloat16),
            pltpu.VMEM((2, channels), jnp.float32),
            pltpu.VMEM((n_col, 2, channels), jnp.float32),
            pltpu.VMEM((2, channels), jnp.float32),
            pltpu.VMEM((n_row, 2, channels), jnp.float32),
            dma((n_col,)), dma((n_col,)), dma((2,)), dma((2,)),
            dma((n_col,)), dma((n_col,)), dma((n_row,)), dma((n_row,)),
        ],
        compiler_params=pltpu.CompilerParams(
            collective_id=0, has_side_effects=True, vmem_limit_bytes=63 * 2**20
        ),
        cost_estimate=pl.CostEstimate(
            flops=2 * tile_h * TILE_W * 9 * channels * channels,
            bytes_accessed=10 * 2**20, transcendentals=0,
        ),
    )(
        latent,
        in_weight.reshape(9 * c_lat, channels),
        in_bias.reshape(1, channels),
        norm_gain.reshape(1, channels),
        norm_shift.reshape(1, channels),
        weight,
        mid_bias.reshape(1, channels),
    )


def solution(mesh):
    placed = (P(None, ("row", "col")), P(), P(), P(), P(), P(), P())
    return jax.shard_map(
        functools.partial(body, mesh.shape["row"], mesh.shape["col"]),
        mesh=mesh, in_specs=placed, out_specs=P("row", "col", None), check_vma=False,
    )
```

```python
import functools

import jax
import jax.numpy as jnp
from jax import lax
from jax.experimental import pallas as pl
from jax.experimental.pallas import tpu as pltpu
from jax.sharding import PartitionSpec as P

GROUPS = 32
TILE_W = 64
EPSILON = 1e-06
LANES = 128
MESH = pl.DeviceIdType.MESH
COLS_PAD = 80
COLS_USED = 72
ROWS_STEP = 8


def front_kernel(
    n_row, n_col, lat_hbm, w_hbm, bias_hbm, gain_hbm, shift_hbm,
    fo_hbm, ss_hbm,
    fo_ref, ss_ref, same_ref, leave_sem,
    lat_ref, w_ref, bias_ref, gain_ref, shift_ref, fetch_sem,
    send, x_ref, xs_ref, part, slot_col, part_row, slot_row,
    send_sem, recv_sem, halo_send, halo_recv, s1_send, s1_recv, s2_send, s2_recv,
):
    row, col = lax.axis_index("row"), lax.axis_index("col")
    fetches = [
        pltpu.make_async_copy(src, dst, fetch_sem.at[i])
        for i, (src, dst) in enumerate([
            (lat_hbm, lat_ref), (w_hbm, w_ref), (bias_hbm, bias_ref), (gain_hbm, gain_ref),
            (shift_hbm, shift_ref),
        ])
    ]
    for fetch in fetches:
        fetch.start()
    c_lat = lat_ref.shape[0]
    breadth = TILE_W * n_col
    rp = lat_ref.shape[1] // breadth
    tile_h = rp * n_col

    barrier = pltpu.get_barrier_semaphore()
    for k in range(1, n_col):
        pl.semaphore_signal(
            barrier, inc=1, device_id=(row, lax.rem(col + k, n_col)), device_id_type=MESH
        )
    for k in range(1, n_row):
        pl.semaphore_signal(
            barrier, inc=1, device_id=(lax.rem(row + k, n_row), col), device_id_type=MESH
        )

    fetches[0].wait()
    zero_tile = jnp.zeros((c_lat, LANES), jnp.float32)
    for r in range(rp):
        tiles = [
            lat_ref[:, r * breadth + t * LANES : r * breadth + (t + 1) * LANES].astype(jnp.float32)
            for t in range(breadth // LANES)
        ]
        for c in range(n_col):
            start = c * TILE_W - 2
            t0 = start // LANES
            off = start - t0 * LANES
            lo = tiles[t0] if t0 >= 0 else zero_tile
            hi = tiles[t0 + 1] if t0 + 1 < len(tiles) else zero_tile
            both = pltpu.roll(jnp.concatenate([lo, hi], axis=1), 2 * LANES - off, 1)
            send[c, r * c_lat : (r + 1) * c_lat, :] = both[:, :LANES].astype(jnp.bfloat16)

    pl.semaphore_wait(barrier, n_col + n_row - 2)

    def rows(first, count):
        return pl.ds(pl.multiple_of(first * c_lat, c_lat), count * c_lat)

    mine = rows(2 + col * rp, rp)
    copies = []
    for k in range(1, n_col):
        target = lax.rem(col + k, n_col)
        copy = pltpu.make_async_remote_copy(
            src_ref=send.at[target],
            dst_ref=x_ref.at[mine],
            send_sem=send_sem.at[k],
            recv_sem=recv_sem.at[k],
            device_id=(row, target),
            device_id_type=MESH,
        )
        copy.start()
        copies.append(copy)
    x_ref[mine, :] = send[col]

    @pl.when(row == 0)
    def _():
        x_ref[rows(0, 2), :] = jnp.zeros((2 * c_lat, LANES), jnp.bfloat16)

    @pl.when(row == n_row - 1)
    def _():
        x_ref[rows(tile_h + 2, 2), :] = jnp.zeros((2 * c_lat, LANES), jnp.bfloat16)

    def spread(i):
        src = x_ref[rows(i, 1), :].astype(jnp.float32)
        for b in range(3):
            moved = src if b == 0 else pltpu.roll(src, LANES - b, 1)
            xs_ref[rows(3 * i + b, 1), :] = moved.astype(jnp.bfloat16)

    def spread_block(source):
        for u in range(rp):
            spread(2 + source * rp + u)

    spread_block(col)
    for k, copy in enumerate(copies):
        copy.wait_recv()
        spread_block(lax.rem(col + n_col - k - 1, n_col))

    down = pltpu.make_async_remote_copy(
        src_ref=x_ref.at[rows(tile_h, 2)],
        dst_ref=x_ref.at[rows(0, 2)],
        send_sem=halo_send.at[0],
        recv_sem=halo_recv.at[0],
        device_id=(jnp.minimum(row + 1, n_row - 1), col),
        device_id_type=MESH,
    )
    up = pltpu.make_async_remote_copy(
        src_ref=x_ref.at[rows(2, 2)],
        dst_ref=x_ref.at[rows(tile_h + 2, 2)],
        send_sem=halo_send.at[1],
        recv_sem=halo_recv.at[1],
        device_id=(jnp.maximum(row - 1, 0), col),
        device_id_type=MESH,
    )

    @pl.when(row < n_row - 1)
    def _():
        down.start()

    @pl.when(row > 0)
    def _():
        up.start()

    fetches[1].wait()
    fetches[2].wait()
    cell = lax.broadcasted_iota(jnp.int32, (COLS_PAD, 1), 0)
    inside = jnp.logical_and(cell >= 1, cell <= TILE_W)
    weight = w_ref[...]
    bias = bias_ref[...]
    channels = weight.shape[1]

    def conv_rows(indices):
        patches = jnp.concatenate([xs_ref[rows(3 * i, 9), :] for i in indices], axis=1)
        prod = lax.dot_general(
            patches, weight, (((0,), (0,)), ((), ())), preferred_element_type=jnp.float32
        )
        outs = []
        for u, i in enumerate(indices):
            out = (prod[u * LANES : u * LANES + COLS_PAD] + bias).astype(jnp.bfloat16)
            fo_ref[i] = out
            outs.append(out)
        return outs

    def stats_rows(indices, carry):
        total, squares = carry
        for out in conv_rows(indices):
            out = jnp.where(inside, out.astype(jnp.float32), 0.0)
            grouped = out.reshape(COLS_PAD // 8, 8, channels)
            total = total + jnp.sum(grouped, axis=0)
            squares = squares + jnp.sum(grouped * grouped, axis=0)
        return total, squares

    def stats_pair(i, carry):
        return stats_rows([2 + 2 * i, 3 + 2 * i], carry)

    zero = jnp.zeros((8, channels), jnp.float32)
    carry = lax.fori_loop(0, (tile_h - 2) // 2, stats_pair, (zero, zero))

    @pl.when(row < n_row - 1)
    def _():
        up.wait_recv()

    @pl.when(row > 0)
    def _():
        down.wait_recv()

    for i in (0, 1, tile_h + 2, tile_h + 3):
        spread(i)
    carry = stats_rows([1, tile_h], carry)
    part[0:1, :] = jnp.sum(carry[0], axis=0, keepdims=True)
    part[1:2, :] = jnp.sum(carry[1], axis=0, keepdims=True)

    for fetch in fetches[3:]:
        fetch.wait()
    firsts = []
    for k in range(1, n_col):
        copy = pltpu.make_async_remote_copy(
            src_ref=part, dst_ref=slot_col.at[k], send_sem=s1_send.at[k],
            recv_sem=s1_recv.at[k],
            device_id=(row, lax.rem(col + k, n_col)), device_id_type=MESH,
        )
        copy.start()
        firsts.append(copy)
    conv_rows([0, tile_h + 1])
    leave_fo = pltpu.make_async_copy(fo_ref, fo_hbm, leave_sem.at[0])
    leave_fo.start()
    width = channels // GROUPS
    left = lax.broadcasted_iota(jnp.int32, (channels, channels), 0) // width
    right = lax.broadcasted_iota(jnp.int32, (channels, channels), 1) // width
    same_ref[...] = (left == right).astype(jnp.bfloat16)
    acc = part[...]
    for k, copy in enumerate(firsts):
        copy.wait_recv()
        acc = acc + slot_col[k + 1]
    part_row[...] = acc
    seconds = []
    for k in range(1, n_row):
        copy = pltpu.make_async_remote_copy(
            src_ref=part_row, dst_ref=slot_row.at[k], send_sem=s2_send.at[k],
            recv_sem=s2_recv.at[k],
            device_id=(lax.rem(row + k, n_row), col), device_id_type=MESH,
        )
        copy.start()
        seconds.append(copy)
    for k, copy in enumerate(seconds):
        copy.wait_recv()
        acc = acc + slot_row[k + 1]

    parts = []
    rest = jnp.concatenate([acc, jnp.zeros((6, channels), jnp.float32)], axis=0)
    for _ in range(3):
        parts.append(rest.astype(jnp.bfloat16).astype(jnp.float32))
        rest = rest - parts[-1]
    parts.append(jnp.zeros_like(rest))
    three = jnp.dot(
        jnp.concatenate(parts, axis=0).astype(jnp.bfloat16), same_ref[...],
        preferred_element_type=jnp.float32,
    )
    summed = three[0:8] + three[8:16] + three[16:24]
    cells = float(tile_h * TILE_W * n_row * n_col * width)
    mean = summed[0:1] / cells
    var = summed[1:2] / cells - mean * mean
    scale = lax.rsqrt(var + EPSILON) * gain_ref[...]
    ss_ref[...] = jnp.zeros_like(ss_ref)
    ss_ref[0:1, :] = scale
    ss_ref[1:2, :] = shift_ref[...] - mean * scale
    leave_ss = pltpu.make_async_copy(ss_ref, ss_hbm, leave_sem.at[1])
    leave_ss.start()
    leave_fo.wait()
    leave_ss.wait()
    for copy in copies + firsts + seconds:
        copy.wait_send()

    @pl.when(row < n_row - 1)
    def _():
        down.wait_send()

    @pl.when(row > 0)
    def _():
        up.wait_send()


def mid_kernel(
    n_row, n_col, fo_hbm, ss_hbm, w_hbm, bias_hbm, out_hbm,
    fo_ref, ss_ref, w_ref, bias_ref, out_ref, even_ref, odd_ref, in_sem, fo_sem, out_sem,
):
    tile_h = out_ref.shape[0]
    blocks = tile_h // ROWS_STEP

    def bring(block):
        part = pl.ds(block * ROWS_STEP + 2, ROWS_STEP)
        return pltpu.make_async_copy(fo_hbm.at[part], fo_ref.at[part], fo_sem.at[block])

    early = [
        pltpu.make_async_copy(ss_hbm, ss_ref, in_sem.at[0]),
        pltpu.make_async_copy(bias_hbm, bias_ref, in_sem.at[1]),
        pltpu.make_async_copy(fo_hbm.at[pl.ds(0, 2)], fo_ref.at[pl.ds(0, 2)], in_sem.at[2]),
        bring(0),
    ]
    fetch_w = pltpu.make_async_copy(w_hbm, w_ref, in_sem.at[3])
    for copy in early + [fetch_w]:
        copy.start()
    for block in range(1, blocks):
        bring(block).start()
    for copy in early:
        copy.wait()
    row, col = lax.axis_index("row"), lax.axis_index("col")
    channels = fo_ref.shape[2]
    scale = ss_ref[0:1, :] * 0.5
    shift = ss_ref[1:2, :] * 0.5
    bias = bias_ref[...]
    cell = lax.broadcasted_iota(jnp.int32, (COLS_USED, 1), 0)
    lowest = jnp.where(col == 0, 1, 0)
    highest = jnp.where(col == n_col - 1, TILE_W, TILE_W + 1)

    def activate(i, act_ref, slot):
        half = fo_ref[i, :COLS_USED].astype(jnp.float32) * scale + shift
        value = half + half * jnp.tanh(half)
        beyond = jnp.logical_or(
            jnp.logical_and(row == 0, i == 0),
            jnp.logical_and(row == n_row - 1, i == tile_h + 1),
        )
        last = jnp.where(beyond, -1, highest)
        value = jnp.where(jnp.logical_and(cell >= lowest, cell <= last), value, 0.0)
        for b in range(3):
            moved = value if b == 0 else pltpu.roll(value, COLS_USED - b, 0)
            act_ref[slot * TILE_W : (slot + 1) * TILE_W, b * channels : (b + 1) * channels] = (
                moved[:TILE_W].astype(jnp.bfloat16)
            )

    for i in range(ROWS_STEP + 2):
        activate(i, even_ref, i)

    rows_m = ROWS_STEP * TILE_W
    fetch_w.wait()

    def leave(block):
        part = pl.ds(block * ROWS_STEP, ROWS_STEP)
        return pltpu.make_async_copy(out_ref.at[part], out_hbm.at[part], out_sem.at[block])

    def two_blocks(step, carry):
        for half_step, (now, later) in enumerate(((even_ref, odd_ref), (odd_ref, even_ref))):
            first = (2 * step + half_step + 1) * ROWS_STEP

            @pl.when(first < tile_h)
            def _(block=2 * step + half_step + 1):
                bring(block).wait()

            later[: 2 * TILE_W, :] = now[rows_m:, :]
            acc = None
            done = 0
            for a in range(3):
                rhs = jnp.concatenate([w_ref[3 * a + b] for b in range(3)], axis=1)
                prod = lax.dot_general(
                    now[a * TILE_W : a * TILE_W + rows_m, :], rhs, (((1,), (1,)), ((), ())),
                    preferred_element_type=jnp.float32,
                )
                upto = ((a + 1) * ROWS_STEP) // 3
                for u in range(done, upto):
                    activate(jnp.minimum(first + 2 + u, tile_h + 1), later, 2 + u)
                done = upto
                acc = prod if acc is None else acc + prod
            out_ref[pl.ds(first - ROWS_STEP, ROWS_STEP)] = (
                (acc + bias).astype(jnp.bfloat16).reshape(ROWS_STEP, TILE_W, channels)
            )
            leave(2 * step + half_step).start()
        return carry

    lax.fori_loop(0, blocks // 2, two_blocks, 0)
    for block in range(blocks):
        leave(block).wait()


def body(n_row, n_col, latent, in_weight, in_bias, norm_gain, norm_shift, mid_weight, mid_bias):
    c_lat = latent.shape[0]
    channels = in_bias.shape[0]
    rp = latent.shape[1] // (TILE_W * n_col)
    tile_h = rp * n_col
    dma = pltpu.SemaphoreType.DMA
    vector = pltpu.VMEM((1, channels), jnp.float32)
    weight = jnp.transpose(mid_weight, (1, 2, 0, 3)).reshape(9, channels, channels)
    act = pltpu.VMEM(((ROWS_STEP + 2) * TILE_W, 3 * channels), jnp.bfloat16)
    out_shape = (tile_h, TILE_W, channels)
    hbm = pl.BlockSpec(memory_space=pltpu.HBM)
    fo_shape = (tile_h + 2, COLS_PAD, channels)
    blocks = tile_h // ROWS_STEP
    fo, ss = pl.pallas_call(
        functools.partial(front_kernel, n_row, n_col),
        out_shape=(
            jax.ShapeDtypeStruct(fo_shape, jnp.bfloat16),
            jax.ShapeDtypeStruct((8, channels), jnp.float32),
        ),
        in_specs=[hbm] * 5,
        out_specs=(hbm, hbm),
        scratch_shapes=[
            pltpu.VMEM(fo_shape, jnp.bfloat16),
            pltpu.VMEM((8, channels), jnp.float32),
            pltpu.VMEM((channels, channels), jnp.bfloat16),
            dma((2,)),
            pltpu.VMEM(latent.shape, jnp.bfloat16),
            pltpu.VMEM((9 * c_lat, channels), jnp.bfloat16),
            vector, vector, vector, dma((5,)),
            pltpu.VMEM((n_col, rp * c_lat, LANES), jnp.bfloat16),
            pltpu.VMEM(((tile_h + 4) * c_lat, LANES), jnp.bfloat16),
            pltpu.VMEM(((tile_h + 4) * 3 * c_lat, LANES), jnp.bfloat16),
            pltpu.VMEM((2, channels), jnp.float32),
            pltpu.VMEM((n_col, 2, channels), jnp.float32),
            pltpu.VMEM((2, channels), jnp.float32),
            pltpu.VMEM((n_row, 2, channels), jnp.float32),
            dma((n_col,)), dma((n_col,)), dma((2,)), dma((2,)),
            dma((n_col,)), dma((n_col,)), dma((n_row,)), dma((n_row,)),
        ],
        compiler_params=pltpu.CompilerParams(
            collective_id=0, has_side_effects=True, vmem_limit_bytes=63 * 2**20
        ),
    )(
        latent,
        in_weight.reshape(9 * c_lat, channels),
        in_bias.reshape(1, channels),
        norm_gain.reshape(1, channels),
        norm_shift.reshape(1, channels),
    )
    return pl.pallas_call(
        functools.partial(mid_kernel, n_row, n_col),
        out_shape=jax.ShapeDtypeStruct(out_shape, jnp.bfloat16),
        in_specs=[hbm] * 4,
        out_specs=hbm,
        scratch_shapes=[
            pltpu.VMEM(fo_shape, jnp.bfloat16),
            pltpu.VMEM((8, channels), jnp.float32),
            pltpu.VMEM(weight.shape, jnp.bfloat16),
            vector,
            pltpu.VMEM(out_shape, jnp.bfloat16),
            act, act, dma((4,)), dma((blocks,)), dma((blocks,)),
        ],
        compiler_params=pltpu.CompilerParams(vmem_limit_bytes=63 * 2**20),
        cost_estimate=pl.CostEstimate(
            flops=2 * tile_h * TILE_W * 9 * channels * channels,
            bytes_accessed=14 * 2**20, transcendentals=0,
        ),
    )(fo, ss, weight, mid_bias.reshape(1, channels))


def solution(mesh):
    placed = (P(None, ("row", "col")), P(), P(), P(), P(), P(), P())
    return jax.shard_map(
        functools.partial(body, mesh.shape["row"], mesh.shape["col"]),
        mesh=mesh, in_specs=placed, out_specs=P("row", "col", None), check_vma=False,
    )
```

```python
import functools

import jax
import jax.numpy as jnp
from jax import lax
from jax.experimental import pallas as pl
from jax.experimental.pallas import tpu as pltpu
from jax.sharding import PartitionSpec as P

GROUPS = 32
TILE_W = 64
EPSILON = 1e-06
LANES = 128
MESH = pl.DeviceIdType.MESH
COLS_PAD = 80
COLS_USED = 72
ROWS_STEP = 8


def front_kernel(
    n_row, n_col, lat_hbm, w_hbm, bias_hbm, gain_hbm, shift_hbm,
    fo_hbm, ss_hbm,
    fo_ref, ss_ref, same_ref, leave_sem,
    lat_ref, w_ref, bias_ref, gain_ref, shift_ref, fetch_sem,
    send, x_ref, xs_ref, part, slot_col, part_row, slot_row,
    send_sem, recv_sem, halo_send, halo_recv, s1_send, s1_recv, s2_send, s2_recv,
):
    row, col = lax.axis_index("row"), lax.axis_index("col")
    fetches = [
        pltpu.make_async_copy(src, dst, fetch_sem.at[i])
        for i, (src, dst) in enumerate([
            (lat_hbm, lat_ref), (w_hbm, w_ref), (bias_hbm, bias_ref), (gain_hbm, gain_ref),
            (shift_hbm, shift_ref),
        ])
    ]
    for fetch in fetches:
        fetch.start()
    c_lat = lat_ref.shape[0]
    breadth = TILE_W * n_col
    rp = lat_ref.shape[1] // breadth
    tile_h = rp * n_col

    barrier = pltpu.get_barrier_semaphore()
    for k in range(1, n_col):
        pl.semaphore_signal(
            barrier, inc=1, device_id=(row, lax.rem(col + k, n_col)), device_id_type=MESH
        )
    for k in range(1, n_row):
        pl.semaphore_signal(
            barrier, inc=1, device_id=(lax.rem(row + k, n_row), col), device_id_type=MESH
        )

    fetches[0].wait()
    zero_tile = jnp.zeros((c_lat, LANES), jnp.float32)
    for r in range(rp):
        tiles = [
            lat_ref[:, r * breadth + t * LANES : r * breadth + (t + 1) * LANES].astype(jnp.float32)
            for t in range(breadth // LANES)
        ]
        for c in range(n_col):
            start = c * TILE_W - 2
            t0 = start // LANES
            off = start - t0 * LANES
            lo = tiles[t0] if t0 >= 0 else zero_tile
            hi = tiles[t0 + 1] if t0 + 1 < len(tiles) else zero_tile
            both = pltpu.roll(jnp.concatenate([lo, hi], axis=1), 2 * LANES - off, 1)
            send[c, r * c_lat : (r + 1) * c_lat, :] = both[:, :LANES].astype(jnp.bfloat16)

    pl.semaphore_wait(barrier, n_col + n_row - 2)

    def rows(first, count):
        return pl.ds(pl.multiple_of(first * c_lat, c_lat), count * c_lat)

    mine = rows(2 + col * rp, rp)
    copies = []
    for k in range(1, n_col):
        target = lax.rem(col + k, n_col)
        copy = pltpu.make_async_remote_copy(
            src_ref=send.at[target],
            dst_ref=x_ref.at[mine],
            send_sem=send_sem.at[k],
            recv_sem=recv_sem.at[k],
            device_id=(row, target),
            device_id_type=MESH,
        )
        copy.start()
        copies.append(copy)
    x_ref[mine, :] = send[col]

    @pl.when(row == 0)
    def _():
        x_ref[rows(0, 2), :] = jnp.zeros((2 * c_lat, LANES), jnp.bfloat16)

    @pl.when(row == n_row - 1)
    def _():
        x_ref[rows(tile_h + 2, 2), :] = jnp.zeros((2 * c_lat, LANES), jnp.bfloat16)

    def spread(i):
        src = x_ref[rows(i, 1), :].astype(jnp.float32)
        for b in range(3):
            moved = src if b == 0 else pltpu.roll(src, LANES - b, 1)
            xs_ref[rows(3 * i + b, 1), :] = moved.astype(jnp.bfloat16)

    def spread_block(source):
        for u in range(rp):
            spread(2 + source * rp + u)

    spread_block(col)
    for k, copy in enumerate(copies):
        copy.wait_recv()
        spread_block(lax.rem(col + n_col - k - 1, n_col))

    down = pltpu.make_async_remote_copy(
        src_ref=x_ref.at[rows(tile_h, 2)],
        dst_ref=x_ref.at[rows(0, 2)],
        send_sem=halo_send.at[0],
        recv_sem=halo_recv.at[0],
        device_id=(jnp.minimum(row + 1, n_row - 1), col),
        device_id_type=MESH,
    )
    up = pltpu.make_async_remote_copy(
        src_ref=x_ref.at[rows(2, 2)],
        dst_ref=x_ref.at[rows(tile_h + 2, 2)],
        send_sem=halo_send.at[1],
        recv_sem=halo_recv.at[1],
        device_id=(jnp.maximum(row - 1, 0), col),
        device_id_type=MESH,
    )

    @pl.when(row < n_row - 1)
    def _():
        down.start()

    @pl.when(row > 0)
    def _():
        up.start()

    fetches[1].wait()
    fetches[2].wait()
    cell = lax.broadcasted_iota(jnp.int32, (COLS_PAD, 1), 0)
    inside = jnp.logical_and(cell >= 1, cell <= TILE_W)
    weight = w_ref[...]
    bias = bias_ref[...]
    channels = weight.shape[1]

    def conv_rows(indices):
        patches = jnp.concatenate([xs_ref[rows(3 * i, 9), :] for i in indices], axis=1)
        prod = lax.dot_general(
            patches, weight, (((0,), (0,)), ((), ())), preferred_element_type=jnp.float32
        )
        outs = []
        for u, i in enumerate(indices):
            out = (prod[u * LANES : u * LANES + COLS_PAD] + bias).astype(jnp.bfloat16)
            fo_ref[i] = out
            outs.append(out)
        return outs

    def stats_rows(indices, carry):
        total, squares = carry
        for out in conv_rows(indices):
            out = jnp.where(inside, out.astype(jnp.float32), 0.0)
            grouped = out.reshape(COLS_PAD // 8, 8, channels)
            total = total + jnp.sum(grouped, axis=0)
            squares = squares + jnp.sum(grouped * grouped, axis=0)
        return total, squares

    def stats_four(i, carry):
        return stats_rows([2 + 4 * i + u for u in range(4)], carry)

    zero = jnp.zeros((8, channels), jnp.float32)
    fours = (tile_h - 2) // 4
    carry = lax.fori_loop(0, fours, stats_four, (zero, zero))
    if 4 * fours < tile_h - 2:
        carry = stats_rows(list(range(2 + 4 * fours, tile_h)), carry)

    @pl.when(row < n_row - 1)
    def _():
        up.wait_recv()

    @pl.when(row > 0)
    def _():
        down.wait_recv()

    for i in (0, 1, tile_h + 2, tile_h + 3):
        spread(i)
    carry = stats_rows([1, tile_h], carry)
    part[0:1, :] = jnp.sum(carry[0], axis=0, keepdims=True)
    part[1:2, :] = jnp.sum(carry[1], axis=0, keepdims=True)

    for fetch in fetches[3:]:
        fetch.wait()
    firsts = []
    for k in range(1, n_col):
        copy = pltpu.make_async_remote_copy(
            src_ref=part, dst_ref=slot_col.at[k], send_sem=s1_send.at[k],
            recv_sem=s1_recv.at[k],
            device_id=(row, lax.rem(col + k, n_col)), device_id_type=MESH,
        )
        copy.start()
        firsts.append(copy)
    conv_rows([0, tile_h + 1])
    leave_fo = pltpu.make_async_copy(fo_ref, fo_hbm, leave_sem.at[0])
    leave_fo.start()
    width = channels // GROUPS
    left = lax.broadcasted_iota(jnp.int32, (channels, channels), 0) // width
    right = lax.broadcasted_iota(jnp.int32, (channels, channels), 1) // width
    same_ref[...] = (left == right).astype(jnp.bfloat16)
    acc = part[...]
    for k, copy in enumerate(firsts):
        copy.wait_recv()
        acc = acc + slot_col[k + 1]
    part_row[...] = acc
    seconds = []
    for k in range(1, n_row):
        copy = pltpu.make_async_remote_copy(
            src_ref=part_row, dst_ref=slot_row.at[k], send_sem=s2_send.at[k],
            recv_sem=s2_recv.at[k],
            device_id=(lax.rem(row + k, n_row), col), device_id_type=MESH,
        )
        copy.start()
        seconds.append(copy)
    for k, copy in enumerate(seconds):
        copy.wait_recv()
        acc = acc + slot_row[k + 1]

    parts = []
    rest = jnp.concatenate([acc, jnp.zeros((6, channels), jnp.float32)], axis=0)
    for _ in range(3):
        parts.append(rest.astype(jnp.bfloat16).astype(jnp.float32))
        rest = rest - parts[-1]
    parts.append(jnp.zeros_like(rest))
    three = jnp.dot(
        jnp.concatenate(parts, axis=0).astype(jnp.bfloat16), same_ref[...],
        preferred_element_type=jnp.float32,
    )
    summed = three[0:8] + three[8:16] + three[16:24]
    cells = float(tile_h * TILE_W * n_row * n_col * width)
    mean = summed[0:1] / cells
    var = summed[1:2] / cells - mean * mean
    scale = lax.rsqrt(var + EPSILON) * gain_ref[...]
    ss_ref[...] = jnp.zeros_like(ss_ref)
    ss_ref[0:1, :] = scale
    ss_ref[1:2, :] = shift_ref[...] - mean * scale
    leave_ss = pltpu.make_async_copy(ss_ref, ss_hbm, leave_sem.at[1])
    leave_ss.start()
    leave_fo.wait()
    leave_ss.wait()
    for copy in copies + firsts + seconds:
        copy.wait_send()

    @pl.when(row < n_row - 1)
    def _():
        down.wait_send()

    @pl.when(row > 0)
    def _():
        up.wait_send()


def mid_kernel(
    n_row, n_col, fo_hbm, ss_hbm, w_hbm, bias_hbm, out_hbm,
    fo_ref, ss_ref, w_ref, bias_ref, out_ref, even_ref, odd_ref, in_sem, fo_sem, out_sem,
):
    tile_h = out_ref.shape[0]
    blocks = tile_h // ROWS_STEP

    def bring(block):
        part = pl.ds(block * ROWS_STEP + 2, ROWS_STEP)
        return pltpu.make_async_copy(fo_hbm.at[part], fo_ref.at[part], fo_sem.at[block])

    early = [
        pltpu.make_async_copy(ss_hbm, ss_ref, in_sem.at[0]),
        pltpu.make_async_copy(bias_hbm, bias_ref, in_sem.at[1]),
        pltpu.make_async_copy(fo_hbm.at[pl.ds(0, 2)], fo_ref.at[pl.ds(0, 2)], in_sem.at[2]),
        bring(0),
    ]
    fetch_w = pltpu.make_async_copy(w_hbm, w_ref, in_sem.at[3])
    for copy in early + [fetch_w]:
        copy.start()
    for block in range(1, blocks):
        bring(block).start()
    for copy in early:
        copy.wait()
    row, col = lax.axis_index("row"), lax.axis_index("col")
    channels = fo_ref.shape[2]
    scale = ss_ref[0:1, :] * 0.5
    shift = ss_ref[1:2, :] * 0.5
    bias = bias_ref[...]
    cell = lax.broadcasted_iota(jnp.int32, (COLS_USED, 1), 0)
    lowest = jnp.where(col == 0, 1, 0)
    highest = jnp.where(col == n_col - 1, TILE_W, TILE_W + 1)

    def activate(i, act_ref, slot):
        half = fo_ref[i, :COLS_USED].astype(jnp.float32) * scale + shift
        value = half + half * jnp.tanh(half)
        beyond = jnp.logical_or(
            jnp.logical_and(row == 0, i == 0),
            jnp.logical_and(row == n_row - 1, i == tile_h + 1),
        )
        last = jnp.where(beyond, -1, highest)
        value = jnp.where(jnp.logical_and(cell >= lowest, cell <= last), value, 0.0)
        for b in range(3):
            moved = value if b == 0 else pltpu.roll(value, COLS_USED - b, 0)
            act_ref[slot * TILE_W : (slot + 1) * TILE_W, b * channels : (b + 1) * channels] = (
                moved[:TILE_W].astype(jnp.bfloat16)
            )

    for i in range(ROWS_STEP + 2):
        activate(i, even_ref, i)

    rows_m = ROWS_STEP * TILE_W
    fetch_w.wait()

    def leave(block):
        part = pl.ds(block * ROWS_STEP, ROWS_STEP)
        return pltpu.make_async_copy(out_ref.at[part], out_hbm.at[part], out_sem.at[block])

    def two_blocks(step, carry):
        for half_step, (now, later) in enumerate(((even_ref, odd_ref), (odd_ref, even_ref))):
            first = (2 * step + half_step + 1) * ROWS_STEP

            @pl.when(first < tile_h)
            def _(block=2 * step + half_step + 1):
                bring(block).wait()

            later[: 2 * TILE_W, :] = now[rows_m:, :]
            acc = None
            done = 0
            for a in range(3):
                rhs = jnp.concatenate([w_ref[3 * a + b] for b in range(3)], axis=1)
                prod = lax.dot_general(
                    now[a * TILE_W : a * TILE_W + rows_m, :], rhs, (((1,), (1,)), ((), ())),
                    preferred_element_type=jnp.float32,
                )
                upto = ((a + 1) * ROWS_STEP) // 3
                for u in range(done, upto):
                    activate(jnp.minimum(first + 2 + u, tile_h + 1), later, 2 + u)
                done = upto
                acc = prod if acc is None else acc + prod
            out_ref[pl.ds(first - ROWS_STEP, ROWS_STEP)] = (
                (acc + bias).astype(jnp.bfloat16).reshape(ROWS_STEP, TILE_W, channels)
            )
            leave(2 * step + half_step).start()
        return carry

    lax.fori_loop(0, blocks // 2, two_blocks, 0)
    for block in range(blocks):
        leave(block).wait()


def body(n_row, n_col, latent, in_weight, in_bias, norm_gain, norm_shift, mid_weight, mid_bias):
    c_lat = latent.shape[0]
    channels = in_bias.shape[0]
    rp = latent.shape[1] // (TILE_W * n_col)
    tile_h = rp * n_col
    dma = pltpu.SemaphoreType.DMA
    vector = pltpu.VMEM((1, channels), jnp.float32)
    weight = jnp.transpose(mid_weight, (1, 2, 0, 3)).reshape(9, channels, channels)
    act = pltpu.VMEM(((ROWS_STEP + 2) * TILE_W, 3 * channels), jnp.bfloat16)
    out_shape = (tile_h, TILE_W, channels)
    hbm = pl.BlockSpec(memory_space=pltpu.HBM)
    fo_shape = (tile_h + 2, COLS_PAD, channels)
    blocks = tile_h // ROWS_STEP
    fo, ss = pl.pallas_call(
        functools.partial(front_kernel, n_row, n_col),
        out_shape=(
            jax.ShapeDtypeStruct(fo_shape, jnp.bfloat16),
            jax.ShapeDtypeStruct((8, channels), jnp.float32),
        ),
        in_specs=[hbm] * 5,
        out_specs=(hbm, hbm),
        scratch_shapes=[
            pltpu.VMEM(fo_shape, jnp.bfloat16),
            pltpu.VMEM((8, channels), jnp.float32),
            pltpu.VMEM((channels, channels), jnp.bfloat16),
            dma((2,)),
            pltpu.VMEM(latent.shape, jnp.bfloat16),
            pltpu.VMEM((9 * c_lat, channels), jnp.bfloat16),
            vector, vector, vector, dma((5,)),
            pltpu.VMEM((n_col, rp * c_lat, LANES), jnp.bfloat16),
            pltpu.VMEM(((tile_h + 4) * c_lat, LANES), jnp.bfloat16),
            pltpu.VMEM(((tile_h + 4) * 3 * c_lat, LANES), jnp.bfloat16),
            pltpu.VMEM((2, channels), jnp.float32),
            pltpu.VMEM((n_col, 2, channels), jnp.float32),
            pltpu.VMEM((2, channels), jnp.float32),
            pltpu.VMEM((n_row, 2, channels), jnp.float32),
            dma((n_col,)), dma((n_col,)), dma((2,)), dma((2,)),
            dma((n_col,)), dma((n_col,)), dma((n_row,)), dma((n_row,)),
        ],
        compiler_params=pltpu.CompilerParams(
            collective_id=0, has_side_effects=True, vmem_limit_bytes=63 * 2**20
        ),
    )(
        latent,
        in_weight.reshape(9 * c_lat, channels),
        in_bias.reshape(1, channels),
        norm_gain.reshape(1, channels),
        norm_shift.reshape(1, channels),
    )
    return pl.pallas_call(
        functools.partial(mid_kernel, n_row, n_col),
        out_shape=jax.ShapeDtypeStruct(out_shape, jnp.bfloat16),
        in_specs=[hbm] * 4,
        out_specs=hbm,
        scratch_shapes=[
            pltpu.VMEM(fo_shape, jnp.bfloat16),
            pltpu.VMEM((8, channels), jnp.float32),
            pltpu.VMEM(weight.shape, jnp.bfloat16),
            vector,
            pltpu.VMEM(out_shape, jnp.bfloat16),
            act, act, dma((4,)), dma((blocks,)), dma((blocks,)),
        ],
        compiler_params=pltpu.CompilerParams(vmem_limit_bytes=63 * 2**20),
        cost_estimate=pl.CostEstimate(
            flops=2 * tile_h * TILE_W * 9 * channels * channels,
            bytes_accessed=14 * 2**20, transcendentals=0,
        ),
    )(fo, ss, weight, mid_bias.reshape(1, channels))


def solution(mesh):
    placed = (P(None, ("row", "col")), P(), P(), P(), P(), P(), P())
    return jax.shard_map(
        functools.partial(body, mesh.shape["row"], mesh.shape["col"]),
        mesh=mesh, in_specs=placed, out_specs=P("row", "col", None), check_vma=False,
    )
```
